32 devices in a mesh: gx: 16 (over z, y, core), gy: 2 (over x).
Axes of the slice: x: 2, y: 2, z: 4, core: 2. Of those that a mesh axis runs over, the one named last changes fastest.
Arguments:
- row_cells: int32 [2, 16, 4096], P('gy', 'gx'), may hold values from 0 to 255
- col_cells: int32 [2, 16, 4096], P('gy', 'gx'), may hold values from 0 to 255
- fracs: float32 [2, 2, 16, 4096], P(None, 'gy', 'gx'), may hold values from 0 to 1
- counts: int32 [2, 16], P('gy', 'gx'), may hold values from 512 to 4096, as said below
- targets: float32 [2, 16, 4096], P('gy', 'gx'), may hold values from -18 to 18
- amplitude: float32 [512, 4096], P('gy', 'gx'), may hold values from 0.5 to 2
- lengthscale: float32 [2], replicated, may hold values from 51.2 to 64
- ridge: float32 [1], replicated, may hold values from 0.5 to 2
Outputs:
- solution: float32 [2, 16, 4096], P('gy', 'gx')
- residual: float32 [2, 16, 4096], P('gy', 'gx')
- relative: float32 [1], replicated
The draws below stay inside these ranges and needn't reach their ends.
Inputs may be any that keep to these rules, and one draw needn't show every extreme that they name: Slots 0 to counts - 1 of a tile are live; some tile holds 4096 live points.
All inputs are finite; a program needn't handle non-finite values.
Results may differ from the reference program's by a relative error of at most 0.0003.
Values sent between devices are 32-bit elements; how exact they have to be, the bound alone decides.
A program may use at most 64 MiB of HBM per device.

```python
import math
import jax
import jax.numpy as jnp

CR = 256
CC = 256
P_SIZE = 4096
HB = 128
NR = 512
NC = 4096
N_GX = 16
N_GY = 2


def draw_counts(key, part):
    total = N_GY * N_GX
    raw_draw = jax.random.randint(jax.random.fold_in(key, 11), (total,), 0, P_SIZE + 1)
    skewed = jnp.maximum(P_SIZE // 8, raw_draw * raw_draw // P_SIZE)
    chosen = jax.random.randint(jax.random.fold_in(key, 17), (), 0, total)
    tile_index = jnp.arange(total, dtype=jnp.int32)
    return jnp.where(tile_index == chosen, P_SIZE, skewed).astype(jnp.int32).reshape(N_GY, N_GX)


def draw_targets(key, part):
    tiles = N_GY * N_GX
    order = (jnp.arange(N_GY)[:, None] * N_GX + jnp.arange(N_GX)[None, :]).astype(jnp.float32)
    rising = 1.0 + 2.0 * order / max(tiles - 1, 1)
    noise = jax.random.truncated_normal(jax.random.fold_in(key, 29), -6.0, 6.0, (N_GY, N_GX, P_SIZE), jnp.float32)
    return noise * rising[:, :, None]


def set_ends(array, rng, least, high):
    longest = array.shape.index(max(array.shape))
    spots = []
    for shift in (0, 1):
        where = [jax.random.randint(jax.random.fold_in(rng, axis), (), 0, length) for axis, length in enumerate(array.shape)]
        where[longest] = (where[longest] + shift) % array.shape[longest]
        spots.append(tuple(where))
    return array.at[spots[0]].set(least).at[spots[1]].set(high)


def block_scale(stream_key, dims, shards, smallest, top_value):
    def one(axis_at, shards_of):
        heights = jax.random.uniform(jax.random.fold_in(jax.random.fold_in(stream_key, 6), axis_at), (shards_of,), jnp.float32, smallest / len(shards), top_value / len(shards))
        return jnp.repeat(jnp.exp(heights), dims[axis_at] // shards_of).reshape((-1,) + (1,) * (len(dims) - axis_at - 1))

    level = one(*shards[0])
    for cut in shards[1:]:
        level = level * one(*cut)
    return level


def setup_inputs(seed: int = 0) -> dict:
    seeds = jax.random.split(jax.random.key(seed), 9)
    row_cells = set_ends(jax.random.randint(seeds[0], (N_GY, N_GX, P_SIZE), 0, CR), jax.random.fold_in(seeds[0], 1), 0, CR - 1).astype(jnp.int32)
    col_cells = set_ends(jax.random.randint(seeds[1], (N_GY, N_GX, P_SIZE), 0, CC), jax.random.fold_in(seeds[1], 1), 0, CC - 1).astype(jnp.int32)
    fracs = jnp.clip(1.0 * jax.random.uniform(seeds[2], (2, N_GY, N_GX, P_SIZE), jnp.float32) ** block_scale(seeds[2], (2, N_GY, N_GX, P_SIZE), ((1, 2), (2, 16)), -0.2, 0.2), 0.0, 1.0)
    counts = draw_counts(jax.random.fold_in(seeds[8], 71), 0)
    targets = draw_targets(jax.random.fold_in(seeds[8], 71), 0)
    amplitude = jnp.clip(jnp.exp(math.log(2.0) - 1.3862944 * jax.random.uniform(seeds[5], (NR, NC), jnp.float32) ** block_scale(seeds[5], (NR, NC), ((0, 2), (1, 16)), -0.2, 0.2)), 0.5, 2.0)
    lengthscale = jnp.clip(jnp.exp(jax.random.uniform(seeds[6], (2,), jnp.float32, math.log(51.2), math.log(64.0))), 51.2, 64.0)
    ridge = jnp.clip(jnp.exp(jax.random.uniform(seeds[7], (1,), jnp.float32, math.log(0.5), math.log(2.0))), 0.5, 2.0)
    return {"row_cells": row_cells, "col_cells": col_cells, "fracs": fracs, "counts": counts, "targets": targets, "amplitude": amplitude, "lengthscale": lengthscale, "ridge": ridge}


def cubic_weights(fraction):
    square = fraction * fraction
    cube = square * fraction
    return (-0.5 * cube + square - 0.5 * fraction,
            1.5 * cube - 2.5 * square + 1.0,
            -1.5 * cube + 2.0 * square + 0.5 * fraction,
            0.5 * cube - 0.5 * square)


def periodic_conv(field, scale, axis):
    length = field.shape[axis]
    offset_idx = jnp.arange(length, dtype=jnp.int32)
    distance = jnp.minimum(offset_idx, length - offset_idx).astype(field.dtype)
    taps = jnp.where(distance <= HB, jnp.exp(-distance * distance / (2.0 * scale * scale)), 0.0)
    spectrum = jnp.fft.rfft(field, axis=axis) * jnp.expand_dims(jnp.fft.rfft(taps), 1 - axis)
    return jnp.fft.irfft(spectrum, n=length, axis=axis).astype(field.dtype)


def reference(row_cells, col_cells, fracs, counts, targets, amplitude, lengthscale, ridge):
    tile_rows = jnp.arange(N_GY, dtype=jnp.int32)[:, None, None]
    tile_cols = jnp.arange(N_GX, dtype=jnp.int32)[None, :, None]
    slot_index = jnp.arange(P_SIZE, dtype=jnp.int32)[None, None, :]
    live_slots = (slot_index < counts[:, :, None]).astype(jnp.float32)
    row_weights = cubic_weights(fracs[0])
    col_weights = cubic_weights(fracs[1])
    row_index = [((tile_rows * CR + row_cells + offset - 1) % NR).astype(jnp.int32) for offset in range(4)]
    col_index = [((tile_cols * CC + col_cells + offset - 1) % NC).astype(jnp.int32) for offset in range(4)]

    def spread(vector):
        flat = jnp.zeros((NR * NC,), jnp.float32)
        for row_step in range(4):
            for col_step in range(4):
                where_to = (row_index[row_step] * NC + col_index[col_step]).reshape(-1)
                amount = vector * live_slots * row_weights[row_step] * col_weights[col_step]
                flat = flat.at[where_to].add(amount.reshape(-1))
        return flat.reshape(NR, NC)

    def gather_back(grid_values):
        total = jnp.zeros(vector_shape, jnp.float32)
        for row_step in range(4):
            for col_step in range(4):
                total = total + row_weights[row_step] * col_weights[col_step] * grid_values[row_index[row_step], col_index[col_step]]
        return total * live_slots

    vector_shape = targets.shape

    def operate(vector):
        field = amplitude * spread(vector)
        smooth = periodic_conv(periodic_conv(field, lengthscale[1], 1), lengthscale[0], 0)
        return gather_back(amplitude * smooth) + ridge[0] * vector

    right_side = targets * live_slots
    norm_start = jnp.sum(right_side * right_side)
    image = operate(right_side)
    step_one = norm_start / jnp.sum(right_side * image)
    solution_one = step_one * right_side
    residual_one = right_side - step_one * image
    norm_mid = jnp.sum(residual_one * residual_one)
    direction = residual_one + (norm_mid / norm_start) * right_side
    image_two = operate(direction)
    step_two = norm_mid / jnp.sum(direction * image_two)
    solution = solution_one + step_two * direction
    residual = residual_one - step_two * image_two
    relative = (jnp.sum(residual * residual) / norm_start).reshape(1)
    return solution, residual, relative
```

```python
import functools

import jax
import jax.numpy as jnp
from jax import lax
from jax.experimental import pallas as pl
from jax.experimental.pallas import tpu as pltpu
from jax.sharding import PartitionSpec as P

HB = 128
CHUNK = 512
MESH = pl.DeviceIdType.MESH
F32 = jnp.float32
BF16 = jnp.bfloat16


def up_to(value, step):
    return (value + step - 1) // step * step


def cubic_weights(fraction):
    square = fraction * fraction
    cube = square * fraction
    return (
        -0.5 * cube + square - 0.5 * fraction,
        1.5 * cube - 2.5 * square + 1.0,
        -1.5 * cube + 2.0 * square + 0.5 * fraction,
        0.5 * cube - 0.5 * square,
    )


def halves(value):
    high = value.astype(BF16)
    return high, (value - high.astype(F32)).astype(BF16)


def product(left, right, dims):
    def part(a, b):
        return lax.dot_general(a, b, (dims, ((), ())), preferred_element_type=F32)

    return part(left[0], right[0]) + part(left[1], right[0]) + part(left[0], right[1])


NN = ((1,), (0,))
NT = ((1,), (1,))


def band(source, target, scale, valid):
    distance = (source - target).astype(F32)
    kept = jnp.where(jnp.abs(distance) <= HB, jnp.exp(-distance * distance / (2.0 * scale * scale)), 0.0)
    return jnp.where(valid, kept, 0.0)


def kernel(
    n_gx, n_gy, rows, cols, slots,
    counts, lengthscale, ridge_ref, row_cells, col_cells, fracs, targets, amp,
    sol_ref, res_ref, rel_ref,
    rt, ct_hi, ct_lo, bc_hi, bc_lo, br_hi, br_lo, amp_ext, acc, vec,
    amp_lo, amp_hi, amp_wide, amp_up, amp_down,
    col_out, col_in, row_out, row_in, sum_out, sum_in,
    amp_send, amp_recv, ex_send, ex_recv, sum_send, sum_recv,
):
    n = n_gx * n_gy
    gx, gy = lax.axis_index("gx"), lax.axis_index("gy")
    me = gx * n_gy + gy
    right = {"gx": lax.rem(gx + 1, n_gx)}
    left = {"gx": lax.rem(gx + n_gx - 1, n_gx)}
    down = {"gy": lax.rem(gy + 1, n_gy)}
    up = {"gy": lax.rem(gy + n_gy - 1, n_gy)}
    er, ec = rt.shape[0], ct_hi.shape[0]
    ct_rows = up_to(cols + 3, 16)
    row_part = row_out.shape[2]

    barrier = pltpu.get_barrier_semaphore()

    def greet(k, carry):
        peer = lax.rem(me + k, n)
        pl.semaphore_signal(
            barrier, inc=1, device_id={"gx": peer // n_gy, "gy": lax.rem(peer, n_gy)}, device_id_type=MESH
        )
        return carry

    lax.fori_loop(1, n, greet, 0)
    pl.semaphore_wait(barrier, n - 1)

    def copy(source, dest, send, recv, to):
        return pltpu.make_async_remote_copy(
            src_ref=source, dst_ref=dest, send_sem=send, recv_sem=recv, device_id=to, device_id_type=MESH
        )

    amp_copies = [
        copy(amp.at[:, pl.ds(0, HB)], amp_hi, amp_send.at[0], amp_recv.at[0], left),
        copy(amp.at[:, pl.ds(cols - HB, HB)], amp_lo, amp_send.at[1], amp_recv.at[1], right),
    ]
    for item in amp_copies:
        item.start()

    source = lax.broadcasted_iota(jnp.int32, bc_hi.shape, 0)
    column = lax.broadcasted_iota(jnp.int32, bc_hi.shape, 1)
    to_left, to_right = column >= ec, column >= ec + 2 * HB
    target = jnp.where(to_right, column - ec - 2 * HB, jnp.where(to_left, column - ec + cols - HB, column))
    valid = (source < cols + 3) & (target < cols + 3)
    target = target + jnp.where(to_right, cols, jnp.where(to_left, -cols, 0))
    bc_hi[...], bc_lo[...] = halves(band(source, target, lengthscale[1], valid))

    source = lax.broadcasted_iota(jnp.int32, br_hi.shape, 1)
    row = lax.broadcasted_iota(jnp.int32, br_hi.shape, 0)
    to_up, to_down = row >= er, row >= er + row_part
    target = jnp.where(to_down, row - er - row_part, jnp.where(to_up, row - er + rows - HB, row))
    valid = (source < rows + 3) & (target < rows + 3)
    target = target + jnp.where(to_down, rows, jnp.where(to_up, -rows, 0))
    br_hi[...], br_lo[...] = halves(band(source, target, lengthscale[0], valid))

    for item in amp_copies:
        item.wait()
    joined = jnp.concatenate([amp_lo[...], amp[...], amp_hi[...]], axis=1)
    amp_wide[...] = pltpu.roll(joined, joined.shape[1] - (HB - 1), 1)[:, :ec]
    amp_rows = [
        copy(amp_wide.at[pl.ds(0, 8)], amp_down, amp_send.at[2], amp_recv.at[2], up),
        copy(amp_wide.at[pl.ds(rows - 8, 8)], amp_up, amp_send.at[3], amp_recv.at[3], down),
    ]
    for item in amp_rows:
        item.start()

    ct_hi[pl.ds(ct_rows, ec - ct_rows), :] = jnp.zeros((ec - ct_rows, slots), BF16)
    ct_lo[pl.ds(ct_rows, ec - ct_rows), :] = jnp.zeros((ec - ct_rows, slots), BF16)

    def chunk(i):
        return pl.ds(pl.multiple_of(i * CHUNK, CHUNK), CHUNK)

    def place(cells, fraction, length):
        index = lax.broadcasted_iota(jnp.int32, (length, CHUNK), 0) - cells
        weights = cubic_weights(fraction)
        out = jnp.zeros((length, CHUNK), F32)
        for offset in range(4):
            out = jnp.where(index == offset, weights[offset], out)
        return out

    def build(i, carry):
        at = chunk(i)
        live = (lax.broadcasted_iota(jnp.int32, (1, CHUNK), 1) + i * CHUNK < counts[0, 0]).astype(F32)
        rt[:, at] = place(row_cells[:, at], fracs[pl.ds(0, 1), at], er) * live
        high, low = halves(place(col_cells[:, at], fracs[pl.ds(1, 1), at], ct_rows))
        ct_hi[pl.ds(0, ct_rows), at] = high
        ct_lo[pl.ds(0, ct_rows), at] = low
        vec[pl.ds(0, 1), at] = targets[:, at] * live
        return carry

    lax.fori_loop(0, slots // CHUNK, build, 0)

    for item in amp_rows:
        item.wait()
    joined = jnp.concatenate([amp_up[...], amp_wide[...], amp_down[...]], axis=0)
    amp_ext[...] = pltpu.roll(joined, joined.shape[0] - 7, 0)[:er]

    ridge = ridge_ref[0]

    def operator_apply(step):
        acc[...] = jnp.zeros_like(acc)

        def spread(i, carry):
            at = chunk(i)
            scaled = halves(rt[:, at] * vec[pl.ds(step, 1), at])
            acc[...] += product(scaled, (ct_hi[:, at], ct_lo[:, at]), NT)
            return carry

        lax.fori_loop(0, slots // CHUNK, spread, 0)
        field = halves(amp_ext[...] * acc[...])
        sides = product(field, (bc_hi[:, pl.ds(ec, 4 * HB)], bc_lo[:, pl.ds(ec, 4 * HB)]), NN)
        col_out[step, 0] = sides[:, : 2 * HB]
        col_out[step, 1] = sides[:, 2 * HB :]
        copies = [
            copy(col_out.at[step, 0], col_in.at[step, 0], ex_send.at[4 * step], ex_recv.at[4 * step], left),
            copy(col_out.at[step, 1], col_in.at[step, 1], ex_send.at[4 * step + 1], ex_recv.at[4 * step + 1], right),
        ]
        for item in copies:
            item.start()
        acc[...] = product(field, (bc_hi[:, pl.ds(0, ec)], bc_lo[:, pl.ds(0, ec)]), NN)
        for item in copies:
            item.wait()
        acc[:, pl.ds(cols - HB, 2 * HB)] += col_in[step, 0]
        acc[:, pl.ds(0, 2 * HB)] += col_in[step, 1]
        across = halves(acc[...])
        count = 2 * row_part
        sides = product((br_hi[pl.ds(er, count), :], br_lo[pl.ds(er, count), :]), across, NN)
        row_out[step, 0] = sides[:row_part]
        row_out[step, 1] = sides[row_part:]
        copies = [
            copy(row_out.at[step, 0], row_in.at[step, 0], ex_send.at[4 * step + 2], ex_recv.at[4 * step + 2], up),
            copy(row_out.at[step, 1], row_in.at[step, 1], ex_send.at[4 * step + 3], ex_recv.at[4 * step + 3], down),
        ]
        for item in copies:
            item.start()
        acc[...] = product((br_hi[pl.ds(0, er), :], br_lo[pl.ds(0, er), :]), across, NN)
        for item in copies:
            item.wait()
        acc[pl.ds(rows - HB, row_part), :] += row_in[step, 0]
        acc[pl.ds(0, row_part), :] += row_in[step, 1]
        grid = halves(amp_ext[...] * acc[...])

        def gather(i, carry):
            at = chunk(i)
            picked = product(grid, (ct_hi[:, at], ct_lo[:, at]), NN)
            found = jnp.sum(picked * rt[:, at], axis=0, keepdims=True)
            vec[pl.ds(step + 1, 1), at] = found + ridge * vec[pl.ds(step, 1), at]
            return carry

        lax.fori_loop(0, slots // CHUNK, gather, 0)

    def lanes(value):
        total = value[:, :128]
        for at in range(1, slots // 128):
            total = total + value[:, at * 128 : (at + 1) * 128]
        return total

    def send_sums(which, values):
        for q, value in enumerate(values):
            sum_out[which, pl.ds(q, 1), :] = lanes(value)
        sum_in[which, me] = sum_out[which]

        def one(k, carry):
            peer = lax.rem(me + k, n)
            copy(
                sum_out.at[which], sum_in.at[which, me], sum_send.at[which], sum_recv.at[which],
                {"gx": peer // n_gy, "gy": lax.rem(peer, n_gy)},
            ).start()
            return carry

        lax.fori_loop(1, n, one, 0)

    def take_sums(which, count):
        others = sum_in.at[which, pl.ds(0, n - 1)]
        pltpu.make_async_copy(others, others, sum_recv.at[which]).wait()
        pltpu.make_async_copy(others, others, sum_send.at[which]).wait()
        total = jnp.sum(sum_in[which], axis=0)
        return [jnp.sum(total[q : q + 1, :]) for q in range(count)]

    sum_out[...] = jnp.zeros_like(sum_out)
    operator_apply(0)
    right_side, image = vec[pl.ds(0, 1), :], vec[pl.ds(1, 1), :]
    send_sums(0, [right_side * right_side, right_side * image])
    operator_apply(1)
    norm_start, first = take_sums(0, 2)
    right_side, image = vec[pl.ds(0, 1), :], vec[pl.ds(1, 1), :]
    step_one = norm_start / first
    residual_one = right_side - step_one * image
    response = image - step_one * vec[pl.ds(2, 1), :]
    send_sums(1, [residual_one * residual_one, residual_one * response])
    norm_mid, second = take_sums(1, 2)
    ratio = norm_mid / norm_start
    direction = residual_one + ratio * right_side
    image_two = response + ratio * image
    step_two = norm_mid / (second - ratio * norm_mid / step_one)
    residual = residual_one - step_two * image_two
    sol_ref[...] = step_one * right_side + step_two * direction
    res_ref[...] = residual
    send_sums(2, [residual * residual])
    (norm_end,) = take_sums(2, 1)
    rel_ref[0] = norm_end / norm_start


def shards(n_gx, n_gy, row_cells, col_cells, fracs, counts, targets, amplitude, lengthscale, ridge):
    rows, cols = amplitude.shape
    slots = targets.shape[2]
    n = n_gx * n_gy
    er, ec = up_to(rows + 3, 16), up_to(cols + 3, 128)
    row_part = up_to(HB + 3, 8)
    vmem = pl.BlockSpec(memory_space=pltpu.VMEM)
    smem = pl.BlockSpec(memory_space=pltpu.SMEM)
    sol, res, rel = pl.pallas_call(
        functools.partial(kernel, n_gx, n_gy, rows, cols, slots),
        out_shape=(
            jax.ShapeDtypeStruct((1, slots), F32),
            jax.ShapeDtypeStruct((1, slots), F32),
            jax.ShapeDtypeStruct((1,), F32),
        ),
        in_specs=[smem] * 3 + [vmem] * 5,
        out_specs=(vmem, vmem, smem),
        scratch_shapes=[
            pltpu.VMEM((er, slots), F32),
            pltpu.VMEM((ec, slots), BF16),
            pltpu.VMEM((ec, slots), BF16),
            pltpu.VMEM((ec, ec + 4 * HB), BF16),
            pltpu.VMEM((ec, ec + 4 * HB), BF16),
            pltpu.VMEM((er + 2 * row_part, er), BF16),
            pltpu.VMEM((er + 2 * row_part, er), BF16),
            pltpu.VMEM((er, ec), F32),
            pltpu.VMEM((er, ec), F32),
            pltpu.VMEM((8, slots), F32),
            pltpu.VMEM((rows, HB), F32),
            pltpu.VMEM((rows, HB), F32),
            pltpu.VMEM((rows, ec), F32),
            pltpu.VMEM((8, ec), F32),
            pltpu.VMEM((8, ec), F32),
            pltpu.VMEM((2, 2, er, 2 * HB), F32),
            pltpu.VMEM((2, 2, er, 2 * HB), F32),
            pltpu.VMEM((2, 2, row_part, ec), F32),
            pltpu.VMEM((2, 2, row_part, ec), F32),
            pltpu.VMEM((3, 8, 128), F32),
            pltpu.VMEM((3, n, 8, 128), F32),
            pltpu.SemaphoreType.DMA((4,)),
            pltpu.SemaphoreType.DMA((4,)),
            pltpu.SemaphoreType.DMA((8,)),
            pltpu.SemaphoreType.DMA((8,)),
            pltpu.SemaphoreType.DMA((3,)),
            pltpu.SemaphoreType.DMA((3,)),
        ],
        compiler_params=pltpu.CompilerParams(
            collective_id=0, has_side_effects=True, vmem_limit_bytes=48 * 1024 * 1024
        ),
    )(
        counts, lengthscale, ridge,
        row_cells[0], col_cells[0], fracs[:, 0, 0], targets[0], amplitude,
    )
    return sol[None], res[None], rel


def solution(mesh):
    placed = (
        P("gy", "gx", None),
        P("gy", "gx", None),
        P(None, "gy", "gx", None),
        P("gy", "gx"),
        P("gy", "gx", None),
        P("gy", "gx"),
        P(),
        P(),
    )
    return jax.shard_map(
        functools.partial(shards, mesh.shape["gx"], mesh.shape["gy"]),
        mesh=mesh,
        in_specs=placed,
        out_specs=(P("gy", "gx", None), P("gy", "gx", None), P()),
        check_vma=False,
    )
```

```python
import functools

import jax
import jax.numpy as jnp
from jax import lax
from jax.experimental import pallas as pl
from jax.experimental.pallas import tpu as pltpu
from jax.sharding import PartitionSpec as P

HB = 128
CHUNK = 2048
BUILD = 512
MESH = pl.DeviceIdType.MESH
F32 = jnp.float32
BF16 = jnp.bfloat16


def up_to(value, step):
    return (value + step - 1) // step * step


def cubic_weights(fraction):
    square = fraction * fraction
    cube = square * fraction
    return (
        -0.5 * cube + square - 0.5 * fraction,
        1.5 * cube - 2.5 * square + 1.0,
        -1.5 * cube + 2.0 * square + 0.5 * fraction,
        0.5 * cube - 0.5 * square,
    )


def halves(value):
    high = value.astype(BF16)
    return high, (value - high.astype(F32)).astype(BF16)


def product(left, right, dims):
    def part(a, b):
        return lax.dot_general(a, b, (dims, ((), ())), preferred_element_type=F32)

    return part(left[0], right[0]) + part(left[1], right[0]) + part(left[0], right[1])


NN = ((1,), (0,))
NT = ((1,), (1,))


def band(source, target, scale, valid):
    distance = (source - target).astype(F32)
    kept = jnp.where(jnp.abs(distance) <= HB, jnp.exp(-distance * distance / (2.0 * scale * scale)), 0.0)
    return jnp.where(valid, kept, 0.0)


def kernel(
    n_gx, n_gy, rows, cols, slots,
    counts, lengthscale, ridge_ref, row_cells, col_cells, fracs, targets, amp,
    sol_ref, res_ref, rel_ref,
    rt, ct_hi, ct_lo, bc_hi, bc_lo, br_hi, br_lo, amp_ext, acc, smooth, vec,
    amp_lo, amp_hi, amp_wide, amp_up, amp_down,
    col_out, col_in, row_out, row_in, sum_out, sum_in,
    amp_send, amp_recv, col_send, col_recv, row_send, row_recv, sum_send, sum_recv,
):
    n = n_gx * n_gy
    gx, gy = lax.axis_index("gx"), lax.axis_index("gy")
    me = gx * n_gy + gy
    right = {"gx": lax.rem(gx + 1, n_gx)}
    left = {"gx": lax.rem(gx + n_gx - 1, n_gx)}
    down = {"gy": lax.rem(gy + 1, n_gy)}
    up = {"gy": lax.rem(gy + n_gy - 1, n_gy)}
    er, ec = rt.shape[0], ct_hi.shape[0]
    ct_rows = up_to(cols + 3, 16)
    row_part = row_out.shape[2] - 8
    side = (br_hi.shape[0] - er) // 2

    half = row_part
    parts = (pl.ds(0, half), pl.ds(half, er - half))

    barrier = pltpu.get_barrier_semaphore()

    def greet(k, carry):
        peer = lax.rem(me + k, n)
        pl.semaphore_signal(
            barrier, inc=1, device_id={"gx": peer // n_gy, "gy": lax.rem(peer, n_gy)}, device_id_type=MESH
        )
        return carry

    lax.fori_loop(1, n, greet, 0)

    def copy(source, dest, send, recv, to):
        return pltpu.make_async_remote_copy(
            src_ref=source, dst_ref=dest, send_sem=send, recv_sem=recv, device_id=to, device_id_type=MESH
        )

    source = lax.broadcasted_iota(jnp.int32, bc_hi.shape, 0)
    column = lax.broadcasted_iota(jnp.int32, bc_hi.shape, 1)
    to_left, to_right = column >= ec, column >= ec + 2 * HB
    target = jnp.where(to_right, column - ec - 2 * HB, jnp.where(to_left, column - ec + cols - HB, column))
    valid = (source < cols + 3) & (target < cols + 3)
    target = target + jnp.where(to_right, cols, jnp.where(to_left, -cols, 0))
    bc_hi[...], bc_lo[...] = halves(band(source, target, lengthscale[1], valid))

    source = lax.broadcasted_iota(jnp.int32, br_hi.shape, 1)
    row = lax.broadcasted_iota(jnp.int32, br_hi.shape, 0)
    to_up, to_down = row >= er, row >= er + side
    target = jnp.where(to_down, row - er - side, jnp.where(to_up, row - er + rows - HB, row))
    valid = (source < rows + 3) & (target < rows + 3)
    target = target + jnp.where(to_down, rows, jnp.where(to_up, -rows, 0))
    br_hi[...], br_lo[...] = halves(band(source, target, lengthscale[0], valid))

    pl.semaphore_wait(barrier, n - 1)
    amp_copies = [
        copy(amp.at[:, pl.ds(0, HB)], amp_hi, amp_send.at[0], amp_recv.at[0], left),
        copy(amp.at[:, pl.ds(cols - HB, HB)], amp_lo, amp_send.at[1], amp_recv.at[1], right),
    ]
    for item in amp_copies:
        item.start()

    ct_hi[pl.ds(ct_rows, ec - ct_rows), :] = jnp.zeros((ec - ct_rows, slots), BF16)
    ct_lo[pl.ds(ct_rows, ec - ct_rows), :] = jnp.zeros((ec - ct_rows, slots), BF16)

    def place(cells, fraction, length):
        index = lax.broadcasted_iota(jnp.int32, (length, BUILD), 0) - cells
        weights = cubic_weights(fraction)
        out = jnp.zeros((length, BUILD), F32)
        for offset in range(4):
            out = jnp.where(index == offset, weights[offset], out)
        return out

    def build(i, carry):
        at = pl.ds(pl.multiple_of(i * BUILD, BUILD), BUILD)
        live = (lax.broadcasted_iota(jnp.int32, (1, BUILD), 1) + i * BUILD < counts[0, 0]).astype(F32)
        rt[:, at] = place(row_cells[:, at], fracs[pl.ds(0, 1), at], er) * live
        high, low = halves(place(col_cells[:, at], fracs[pl.ds(1, 1), at], ct_rows))
        ct_hi[pl.ds(0, ct_rows), at] = high
        ct_lo[pl.ds(0, ct_rows), at] = low
        vec[pl.ds(0, 1), at] = targets[:, at] * live
        return carry

    builds = slots // BUILD
    lax.fori_loop(0, builds // 2, build, 0)

    for item in amp_copies:
        item.wait()
    joined = jnp.concatenate([amp_lo[...], amp[...], amp_hi[...]], axis=1)
    amp_wide[...] = pltpu.roll(joined, joined.shape[1] - (HB - 1), 1)[:, :ec]
    amp_rows = [
        copy(amp_wide.at[pl.ds(0, 8)], amp_down, amp_send.at[2], amp_recv.at[2], up),
        copy(amp_wide.at[pl.ds(rows - 8, 8)], amp_up, amp_send.at[3], amp_recv.at[3], down),
    ]
    for item in amp_rows:
        item.start()

    lax.fori_loop(builds // 2, builds, build, 0)

    for item in amp_rows:
        item.wait()
    joined = jnp.concatenate([amp_up[...], amp_wide[...], amp_down[...]], axis=0)
    amp_ext[...] = pltpu.roll(joined, joined.shape[0] - 7, 0)[:er]

    ridge = ridge_ref[0]
    chunks = [pl.ds(at, CHUNK) for at in range(0, slots, CHUNK)]

    def pack(edge):
        total = edge[:8]
        for i in range(1, edge.shape[0] // 8):
            total = total + pltpu.roll(edge[8 * i : 8 * i + 8], 3 * i, 1)
        return total

    def unpack(packed, length):
        first = lax.broadcasted_iota(jnp.int32, packed.shape, 1) < 3
        return jnp.concatenate(
            [jnp.where(first, pltpu.roll(packed, 128 - 3 * i, 1) if i else packed, 0.0) for i in range(length // 8)],
            axis=0,
        )

    def operator_apply(step):
        col_copies = []

        def spread(h):
            total = None
            for at in chunks:
                scaled = halves(rt[parts[h], at] * vec[pl.ds(step, 1), at])
                term = product(scaled, (ct_hi[:, at], ct_lo[:, at]), NT)
                total = term if total is None else total + term
            field = halves(amp_ext[parts[h], :] * total)
            sides = product(field, (bc_hi[:, pl.ds(ec, 4 * HB)], bc_lo[:, pl.ds(ec, 4 * HB)]), NN)
            length = sides.shape[0]
            for d, to in enumerate((left, right)):
                out = col_out.at[step, h, d]
                out[pl.ds(0, length), :] = sides[:, 2 * HB * d : 2 * HB * d + HB]
                out[pl.ds(length, 8), :] = pack(sides[:, 2 * HB * d + HB : 2 * HB * (d + 1)])
                sem = 4 * step + 2 * h + d
                item = copy(out, col_in.at[step, h, d], col_send.at[sem], col_recv.at[sem], to)
                item.start()
                col_copies.append(item)
            acc[parts[h], :] = product(field, (bc_hi[:, pl.ds(0, ec)], bc_lo[:, pl.ds(0, ec)]), NN)

        def collect(h):
            length = half if h == 0 else er - half
            for d in range(2):
                col_copies[2 * h + d].wait()
                start = cols - HB if d == 0 else 0
                got = col_in.at[step, h, d]
                acc[parts[h], pl.ds(start, HB)] += got[pl.ds(0, length), :]
                acc[parts[h], pl.ds(start + HB, HB)] += unpack(got[pl.ds(length, 8), :], length)

        def send_rows(d, to, low, count):
            taps = (br_hi[pl.ds(er + side * d, side), pl.ds(low, count)], br_lo[pl.ds(er + side * d, side), pl.ds(low, count)])
            piece = product(taps, halves(acc[pl.ds(low, count), :]), NN)
            out = row_out.at[step, d]
            out[pl.ds(0, row_part), :] = piece[:row_part, :cols]
            out[pl.ds(row_part, 8), :] = jnp.zeros((8, cols), F32)
            out[pl.ds(row_part, 8), pl.ds(0, 128)] = pack(piece[:row_part, cols:])
            item = copy(out, row_in.at[step, d], row_send.at[2 * step + d], row_recv.at[2 * step + d], to)
            item.start()
            return item

        def take_rows(d, item):
            item.wait()
            at = pl.ds(rows - HB, row_part) if d == 0 else pl.ds(0, row_part)
            got = row_in.at[step, d]
            smooth[at, pl.ds(0, cols)] += got[pl.ds(0, row_part), :]
            smooth[at, pl.ds(cols, 128)] += unpack(got[pl.ds(row_part, 8), pl.ds(0, 128)], row_part)

        def gather(h):
            grid = halves(amp_ext[parts[h], :] * smooth[parts[h], :])
            for at in chunks:
                picked = product(grid, (ct_hi[:, at], ct_lo[:, at]), NN)
                found = jnp.sum(picked * rt[parts[h], at], axis=0, keepdims=True)
                if h == 1:
                    vec[pl.ds(step + 1, 1), at] = found + ridge * vec[pl.ds(step, 1), at]
                else:
                    vec[pl.ds(step + 1, 1), at] += found

        spread(0)
        spread(1)
        collect(0)
        sent_up = send_rows(0, up, 0, half)
        collect(1)
        sent_down = send_rows(1, down, rows - HB, er - (rows - HB))
        smooth[...] = product((br_hi[pl.ds(0, er), :], br_lo[pl.ds(0, er), :]), halves(acc[...]), NN)
        take_rows(0, sent_up)
        gather(1)
        take_rows(1, sent_down)
        gather(0)

    def lanes(value):
        total = value[:, :128]
        for at in range(1, slots // 128):
            total = total + value[:, at * 128 : (at + 1) * 128]
        return total

    def send_sums(which, values):
        for q, value in enumerate(values):
            sum_out[which, pl.ds(q, 1), :] = lanes(value)
        sum_in[which, me] = sum_out[which]

        def one(k, carry):
            peer = lax.rem(me + k, n)
            copy(
                sum_out.at[which], sum_in.at[which, me], sum_send.at[which], sum_recv.at[which],
                {"gx": peer // n_gy, "gy": lax.rem(peer, n_gy)},
            ).start()
            return carry

        lax.fori_loop(1, n, one, 0)

    def take_sums(which, count):
        others = sum_in.at[which, pl.ds(0, n - 1)]
        pltpu.make_async_copy(others, others, sum_recv.at[which]).wait()
        pltpu.make_async_copy(others, others, sum_send.at[which]).wait()
        total = jnp.sum(sum_in[which], axis=0)
        return [jnp.sum(total[q : q + 1, :]) for q in range(count)]

    sum_out[...] = jnp.zeros_like(sum_out)
    operator_apply(0)
    right_side, image = vec[pl.ds(0, 1), :], vec[pl.ds(1, 1), :]
    send_sums(0, [right_side * right_side, right_side * image])
    operator_apply(1)
    norm_start, first = take_sums(0, 2)
    right_side, image = vec[pl.ds(0, 1), :], vec[pl.ds(1, 1), :]
    step_one = norm_start / first
    residual_one = right_side - step_one * image
    response = image - step_one * vec[pl.ds(2, 1), :]
    send_sums(1, [residual_one * residual_one, residual_one * response])
    norm_mid, second = take_sums(1, 2)
    ratio = norm_mid / norm_start
    direction = residual_one + ratio * right_side
    image_two = response + ratio * image
    step_two = norm_mid / (second - ratio * norm_mid / step_one)
    residual = residual_one - step_two * image_two
    sol_ref[...] = step_one * right_side + step_two * direction
    res_ref[...] = residual
    send_sums(2, [residual * residual])
    (norm_end,) = take_sums(2, 1)
    rel_ref[0] = norm_end / norm_start


def shards(n_gx, n_gy, row_cells, col_cells, fracs, counts, targets, amplitude, lengthscale, ridge):
    rows, cols = amplitude.shape
    slots = targets.shape[2]
    n = n_gx * n_gy
    er, ec = up_to(rows + 3, 16), up_to(cols + 3, 128)
    row_part = up_to(HB + 3, 8)
    vmem = pl.BlockSpec(memory_space=pltpu.VMEM)
    smem = pl.BlockSpec(memory_space=pltpu.SMEM)
    sol, res, rel = pl.pallas_call(
        functools.partial(kernel, n_gx, n_gy, rows, cols, slots),
        out_shape=(
            jax.ShapeDtypeStruct((1, slots), F32),
            jax.ShapeDtypeStruct((1, slots), F32),
            jax.ShapeDtypeStruct((1,), F32),
        ),
        in_specs=[smem] * 3 + [vmem] * 5,
        out_specs=(vmem, vmem, smem),
        scratch_shapes=[
            pltpu.VMEM((er, slots), F32),
            pltpu.VMEM((ec, slots), BF16),
            pltpu.VMEM((ec, slots), BF16),
            pltpu.VMEM((ec, ec + 4 * HB), BF16),
            pltpu.VMEM((ec, ec + 4 * HB), BF16),
            pltpu.VMEM((er + 2 * up_to(HB + 3, 16), er), BF16),
            pltpu.VMEM((er + 2 * up_to(HB + 3, 16), er), BF16),
            pltpu.VMEM((er, ec), F32),
            pltpu.VMEM((er, ec), F32),
            pltpu.VMEM((er, ec), F32),
            pltpu.VMEM((8, slots), F32),
            pltpu.VMEM((rows, HB), F32),
            pltpu.VMEM((rows, HB), F32),
            pltpu.VMEM((rows, ec), F32),
            pltpu.VMEM((8, ec), F32),
            pltpu.VMEM((8, ec), F32),
            pltpu.VMEM((2, 2, 2, max(row_part, er - row_part) + 8, HB), F32),
            pltpu.VMEM((2, 2, 2, max(row_part, er - row_part) + 8, HB), F32),
            pltpu.VMEM((2, 2, row_part + 8, cols), F32),
            pltpu.VMEM((2, 2, row_part + 8, cols), F32),
            pltpu.VMEM((3, 8, 128), F32),
            pltpu.VMEM((3, n, 8, 128), F32),
            pltpu.SemaphoreType.DMA((4,)),
            pltpu.SemaphoreType.DMA((4,)),
            pltpu.SemaphoreType.DMA((8,)),
            pltpu.SemaphoreType.DMA((8,)),
            pltpu.SemaphoreType.DMA((4,)),
            pltpu.SemaphoreType.DMA((4,)),
            pltpu.SemaphoreType.DMA((3,)),
            pltpu.SemaphoreType.DMA((3,)),
        ],
        compiler_params=pltpu.CompilerParams(
            collective_id=0, has_side_effects=True, vmem_limit_bytes=48 * 1024 * 1024
        ),
    )(
        counts, lengthscale, ridge,
        row_cells[0], col_cells[0], fracs[:, 0, 0], targets[0], amplitude,
    )
    return sol[None], res[None], rel


def solution(mesh):
    placed = (
        P("gy", "gx", None),
        P("gy", "gx", None),
        P(None, "gy", "gx", None),
        P("gy", "gx"),
        P("gy", "gx", None),
        P("gy", "gx"),
        P(),
        P(),
    )
    return jax.shard_map(
        functools.partial(shards, mesh.shape["gx"], mesh.shape["gy"]),
        mesh=mesh,
        in_specs=placed,
        out_specs=(P("gy", "gx", None), P("gy", "gx", None), P()),
        check_vma=False,
    )
```

```python
import functools

import jax
import jax.numpy as jnp
from jax import lax
from jax.experimental import pallas as pl
from jax.experimental.pallas import tpu as pltpu
from jax.sharding import PartitionSpec as P

HB = 128
CHUNK = 4096
BUILD = 512
MESH = pl.DeviceIdType.MESH
F32 = jnp.float32
BF16 = jnp.bfloat16


def up_to(value, step):
    return (value + step - 1) // step * step


def cubic_weights(fraction):
    square = fraction * fraction
    cube = square * fraction
    return (
        -0.5 * cube + square - 0.5 * fraction,
        1.5 * cube - 2.5 * square + 1.0,
        -1.5 * cube + 2.0 * square + 0.5 * fraction,
        0.5 * cube - 0.5 * square,
    )


def halves(value):
    high = value.astype(BF16)
    return high, (value - high.astype(F32)).astype(BF16)


def product(left, right, dims):
    def part(a, b):
        return lax.dot_general(a, b, (dims, ((), ())), preferred_element_type=F32)

    return part(left[0], right[0]) + part(left[1], right[0]) + part(left[0], right[1])


NN = ((1,), (0,))
NT = ((1,), (1,))


def band(source, target, scale, valid):
    distance = (source - target).astype(F32)
    kept = jnp.where(jnp.abs(distance) <= HB, jnp.exp(-distance * distance / (2.0 * scale * scale)), 0.0)
    return jnp.where(valid, kept, 0.0)


def kernel(
    n_gx, n_gy, rows, cols, slots,
    counts, lengthscale, ridge_ref, row_cells, col_cells, fracs, targets, amp,
    sol_ref, res_ref, rel_ref,
    rt, ct_hi, ct_lo, bc_hi, bc_lo, br_hi, br_lo, amp_ext, acc, smooth, vec,
    amp_lo, amp_hi, amp_wide, amp_up, amp_down,
    col_out, col_in, row_out, row_in, sum_out, sum_in,
    amp_send, amp_recv, col_send, col_recv, row_send, row_recv, sum_send, sum_recv,
):
    n = n_gx * n_gy
    gx, gy = lax.axis_index("gx"), lax.axis_index("gy")
    me = gx * n_gy + gy
    right = {"gx": lax.rem(gx + 1, n_gx)}
    left = {"gx": lax.rem(gx + n_gx - 1, n_gx)}
    down = {"gy": lax.rem(gy + 1, n_gy)}
    up = {"gy": lax.rem(gy + n_gy - 1, n_gy)}
    er, ec = rt.shape[0], ct_hi.shape[0]
    ct_rows = up_to(cols + 3, 16)
    row_part = row_out.shape[2] - 8
    side = (br_hi.shape[0] - er) // 2

    half = row_part
    parts = (pl.ds(0, half), pl.ds(half, er - half))

    barrier = pltpu.get_barrier_semaphore()

    def greet(k, carry):
        peer = lax.rem(me + k, n)
        pl.semaphore_signal(
            barrier, inc=1, device_id={"gx": peer // n_gy, "gy": lax.rem(peer, n_gy)}, device_id_type=MESH
        )
        return carry

    lax.fori_loop(1, n, greet, 0)

    def copy(source, dest, send, recv, to):
        return pltpu.make_async_remote_copy(
            src_ref=source, dst_ref=dest, send_sem=send, recv_sem=recv, device_id=to, device_id_type=MESH
        )

    source = lax.broadcasted_iota(jnp.int32, bc_hi.shape, 0)
    column = lax.broadcasted_iota(jnp.int32, bc_hi.shape, 1)
    to_left, to_right = column >= ec, column >= ec + 2 * HB
    target = jnp.where(to_right, column - ec - 2 * HB, jnp.where(to_left, column - ec + cols - HB, column))
    valid = (source < cols + 3) & (target < cols + 3)
    target = target + jnp.where(to_right, cols, jnp.where(to_left, -cols, 0))
    bc_hi[...], bc_lo[...] = halves(band(source, target, lengthscale[1], valid))

    source = lax.broadcasted_iota(jnp.int32, br_hi.shape, 1)
    row = lax.broadcasted_iota(jnp.int32, br_hi.shape, 0)
    to_up, to_down = row >= er, row >= er + side
    target = jnp.where(to_down, row - er - side, jnp.where(to_up, row - er + rows - HB, row))
    valid = (source < rows + 3) & (target < rows + 3)
    target = target + jnp.where(to_down, rows, jnp.where(to_up, -rows, 0))
    br_hi[...], br_lo[...] = halves(band(source, target, lengthscale[0], valid))

    pl.semaphore_wait(barrier, n - 1)
    amp_copies = [
        copy(amp.at[:, pl.ds(0, HB)], amp_hi, amp_send.at[0], amp_recv.at[0], left),
        copy(amp.at[:, pl.ds(cols - HB, HB)], amp_lo, amp_send.at[1], amp_recv.at[1], right),
    ]
    for item in amp_copies:
        item.start()

    ct_hi[pl.ds(ct_rows, ec - ct_rows), :] = jnp.zeros((ec - ct_rows, slots), BF16)
    ct_lo[pl.ds(ct_rows, ec - ct_rows), :] = jnp.zeros((ec - ct_rows, slots), BF16)

    def place(cells, fraction, length):
        index = lax.broadcasted_iota(jnp.int32, (length, BUILD), 0) - cells
        weights = cubic_weights(fraction)
        out = jnp.zeros((length, BUILD), F32)
        for offset in range(4):
            out = jnp.where(index == offset, weights[offset], out)
        return out

    def build(i, carry):
        at = pl.ds(pl.multiple_of(i * BUILD, BUILD), BUILD)
        live = (lax.broadcasted_iota(jnp.int32, (1, BUILD), 1) + i * BUILD < counts[0, 0]).astype(F32)
        rt[:, at] = place(row_cells[:, at], fracs[pl.ds(0, 1), at], er) * live
        high, low = halves(place(col_cells[:, at], fracs[pl.ds(1, 1), at], ct_rows))
        ct_hi[pl.ds(0, ct_rows), at] = high
        ct_lo[pl.ds(0, ct_rows), at] = low
        vec[pl.ds(0, 1), at] = targets[:, at] * live
        return carry

    builds = slots // BUILD
    lax.fori_loop(0, builds // 2, build, 0)

    for item in amp_copies:
        item.wait()
    joined = jnp.concatenate([amp_lo[...], amp[...], amp_hi[...]], axis=1)
    amp_wide[...] = pltpu.roll(joined, joined.shape[1] - (HB - 1), 1)[:, :ec]
    amp_rows = [
        copy(amp_wide.at[pl.ds(0, 8)], amp_down, amp_send.at[2], amp_recv.at[2], up),
        copy(amp_wide.at[pl.ds(rows - 8, 8)], amp_up, amp_send.at[3], amp_recv.at[3], down),
    ]
    for item in amp_rows:
        item.start()

    lax.fori_loop(builds // 2, builds, build, 0)

    for item in amp_rows:
        item.wait()
    joined = jnp.concatenate([amp_up[...], amp_wide[...], amp_down[...]], axis=0)
    amp_ext[...] = pltpu.roll(joined, joined.shape[0] - 7, 0)[:er]

    ridge = ridge_ref[0]
    chunks = [pl.ds(at, CHUNK) for at in range(0, slots, CHUNK)]

    def pack(edge):
        total = edge[:8]
        for i in range(1, edge.shape[0] // 8):
            total = total + pltpu.roll(edge[8 * i : 8 * i + 8], 3 * i, 1)
        return total

    def unpack(packed, length):
        first = lax.broadcasted_iota(jnp.int32, packed.shape, 1) < 3
        return jnp.concatenate(
            [jnp.where(first, pltpu.roll(packed, 128 - 3 * i, 1) if i else packed, 0.0) for i in range(length // 8)],
            axis=0,
        )

    def operator_apply(step):
        col_copies = []

        def spread(h):
            total = None
            for at in chunks:
                scaled = halves(rt[parts[h], at] * vec[pl.ds(step, 1), at])
                term = product(scaled, (ct_hi[:, at], ct_lo[:, at]), NT)
                total = term if total is None else total + term
            field = halves(amp_ext[parts[h], :] * total)
            sides = product(field, (bc_hi[:, pl.ds(ec, 4 * HB)], bc_lo[:, pl.ds(ec, 4 * HB)]), NN)
            length = sides.shape[0]
            for d, to in enumerate((left, right)):
                out = col_out.at[step, h, d]
                out[pl.ds(0, length), :] = sides[:, 2 * HB * d : 2 * HB * d + HB]
                out[pl.ds(length, 8), :] = pack(sides[:, 2 * HB * d + HB : 2 * HB * (d + 1)])
                sem = 4 * step + 2 * h + d
                item = copy(out, col_in.at[step, h, d], col_send.at[sem], col_recv.at[sem], to)
                item.start()
                col_copies.append(item)
            acc[parts[h], :] = product(field, (bc_hi[:, pl.ds(0, ec)], bc_lo[:, pl.ds(0, ec)]), NN)

        def collect(h):
            length = half if h == 0 else er - half
            for d in range(2):
                col_copies[2 * h + d].wait()
                start = cols - HB if d == 0 else 0
                got = col_in.at[step, h, d]
                acc[parts[h], pl.ds(start, HB)] += got[pl.ds(0, length), :]
                acc[parts[h], pl.ds(start + HB, HB)] += unpack(got[pl.ds(length, 8), :], length)

        def send_rows(d, to, low, count):
            taps = (br_hi[pl.ds(er + side * d, side), pl.ds(low, count)], br_lo[pl.ds(er + side * d, side), pl.ds(low, count)])
            piece = product(taps, halves(acc[pl.ds(low, count), :]), NN)
            out = row_out.at[step, d]
            out[pl.ds(0, row_part), :] = piece[:row_part, :cols]
            out[pl.ds(row_part, 8), :] = jnp.zeros((8, cols), F32)
            out[pl.ds(row_part, 8), pl.ds(0, 128)] = pack(piece[:row_part, cols:])
            item = copy(out, row_in.at[step, d], row_send.at[2 * step + d], row_recv.at[2 * step + d], to)
            item.start()
            return item

        def take_rows(d, item):
            item.wait()
            at = pl.ds(rows - HB, row_part) if d == 0 else pl.ds(0, row_part)
            got = row_in.at[step, d]
            smooth[at, pl.ds(0, cols)] += got[pl.ds(0, row_part), :]
            smooth[at, pl.ds(cols, 128)] += unpack(got[pl.ds(row_part, 8), pl.ds(0, 128)], row_part)

        def gather(h):
            grid = halves(amp_ext[parts[h], :] * smooth[parts[h], :])
            for at in chunks:
                picked = product(grid, (ct_hi[:, at], ct_lo[:, at]), NN)
                found = jnp.sum(picked * rt[parts[h], at], axis=0, keepdims=True)
                if h == 1:
                    vec[pl.ds(step + 1, 1), at] = found + ridge * vec[pl.ds(step, 1), at]
                else:
                    vec[pl.ds(step + 1, 1), at] += found

        spread(0)
        spread(1)
        collect(0)
        sent_up = send_rows(0, up, 0, half)
        collect(1)
        sent_down = send_rows(1, down, rows - HB, er - (rows - HB))
        smooth[...] = product((br_hi[pl.ds(0, er), :], br_lo[pl.ds(0, er), :]), halves(acc[...]), NN)
        take_rows(0, sent_up)
        gather(1)
        take_rows(1, sent_down)
        gather(0)

    def lanes(value):
        total = value[:, :128]
        for at in range(1, slots // 128):
            total = total + value[:, at * 128 : (at + 1) * 128]
        return total

    def send_sums(which, values):
        for q, value in enumerate(values):
            sum_out[which, pl.ds(q, 1), :] = lanes(value)
        sum_in[which, me] = sum_out[which]

        def one(k, carry):
            peer = lax.rem(me + k, n)
            copy(
                sum_out.at[which], sum_in.at[which, me], sum_send.at[which], sum_recv.at[which],
                {"gx": peer // n_gy, "gy": lax.rem(peer, n_gy)},
            ).start()
            return carry

        lax.fori_loop(1, n, one, 0)

    def take_sums(which, count):
        others = sum_in.at[which, pl.ds(0, n - 1)]
        pltpu.make_async_copy(others, others, sum_recv.at[which]).wait()
        pltpu.make_async_copy(others, others, sum_send.at[which]).wait()
        total = jnp.sum(sum_in[which], axis=0)
        return [jnp.sum(total[q : q + 1, :]) for q in range(count)]

    sum_out[...] = jnp.zeros_like(sum_out)
    operator_apply(0)
    right_side, image = vec[pl.ds(0, 1), :], vec[pl.ds(1, 1), :]
    send_sums(0, [right_side * right_side, right_side * image])
    operator_apply(1)
    norm_start, first = take_sums(0, 2)
    right_side, image = vec[pl.ds(0, 1), :], vec[pl.ds(1, 1), :]
    step_one = norm_start / first
    residual_one = right_side - step_one * image
    response = image - step_one * vec[pl.ds(2, 1), :]
    send_sums(1, [residual_one * residual_one, residual_one * response])
    norm_mid, second = take_sums(1, 2)
    ratio = norm_mid / norm_start
    direction = residual_one + ratio * right_side
    image_two = response + ratio * image
    step_two = norm_mid / (second - ratio * norm_mid / step_one)
    residual = residual_one - step_two * image_two
    sol_ref[...] = step_one * right_side + step_two * direction
    res_ref[...] = residual
    send_sums(2, [residual * residual])
    (norm_end,) = take_sums(2, 1)
    rel_ref[0] = norm_end / norm_start


def shards(n_gx, n_gy, row_cells, col_cells, fracs, counts, targets, amplitude, lengthscale, ridge):
    rows, cols = amplitude.shape
    slots = targets.shape[2]
    n = n_gx * n_gy
    er, ec = up_to(rows + 3, 16), up_to(cols + 3, 128)
    row_part = up_to(HB + 3, 8)
    vmem = pl.BlockSpec(memory_space=pltpu.VMEM)
    smem = pl.BlockSpec(memory_space=pltpu.SMEM)
    sol, res, rel = pl.pallas_call(
        functools.partial(kernel, n_gx, n_gy, rows, cols, slots),
        out_shape=(
            jax.ShapeDtypeStruct((1, slots), F32),
            jax.ShapeDtypeStruct((1, slots), F32),
            jax.ShapeDtypeStruct((1,), F32),
        ),
        in_specs=[smem] * 3 + [vmem] * 5,
        out_specs=(vmem, vmem, smem),
        scratch_shapes=[
            pltpu.VMEM((er, slots), F32),
            pltpu.VMEM((ec, slots), BF16),
            pltpu.VMEM((ec, slots), BF16),
            pltpu.VMEM((ec, ec + 4 * HB), BF16),
            pltpu.VMEM((ec, ec + 4 * HB), BF16),
            pltpu.VMEM((er + 2 * up_to(HB + 3, 16), er), BF16),
            pltpu.VMEM((er + 2 * up_to(HB + 3, 16), er), BF16),
            pltpu.VMEM((er, ec), F32),
            pltpu.VMEM((er, ec), F32),
            pltpu.VMEM((er, ec), F32),
            pltpu.VMEM((8, slots), F32),
            pltpu.VMEM((rows, HB), F32),
            pltpu.VMEM((rows, HB), F32),
            pltpu.VMEM((rows, ec), F32),
            pltpu.VMEM((8, ec), F32),
            pltpu.VMEM((8, ec), F32),
            pltpu.VMEM((2, 2, 2, max(row_part, er - row_part) + 8, HB), F32),
            pltpu.VMEM((2, 2, 2, max(row_part, er - row_part) + 8, HB), F32),
            pltpu.VMEM((2, 2, row_part + 8, cols), F32),
            pltpu.VMEM((2, 2, row_part + 8, cols), F32),
            pltpu.VMEM((3, 8, 128), F32),
            pltpu.VMEM((3, n, 8, 128), F32),
            pltpu.SemaphoreType.DMA((4,)),
            pltpu.SemaphoreType.DMA((4,)),
            pltpu.SemaphoreType.DMA((8,)),
            pltpu.SemaphoreType.DMA((8,)),
            pltpu.SemaphoreType.DMA((4,)),
            pltpu.SemaphoreType.DMA((4,)),
            pltpu.SemaphoreType.DMA((3,)),
            pltpu.SemaphoreType.DMA((3,)),
        ],
        compiler_params=pltpu.CompilerParams(
            collective_id=0, has_side_effects=True, vmem_limit_bytes=48 * 1024 * 1024
        ),
    )(
        counts, lengthscale, ridge,
        row_cells[0], col_cells[0], fracs[:, 0, 0], targets[0], amplitude,
    )
    return sol[None], res[None], rel


def solution(mesh):
    placed = (
        P("gy", "gx", None),
        P("gy", "gx", None),
        P(None, "gy", "gx", None),
        P("gy", "gx"),
        P("gy", "gx", None),
        P("gy", "gx"),
        P(),
        P(),
    )
    return jax.shard_map(
        functools.partial(shards, mesh.shape["gx"], mesh.shape["gy"]),
        mesh=mesh,
        in_specs=placed,
        out_specs=(P("gy", "gx", None), P("gy", "gx", None), P()),
        check_vma=False,
    )
```
